256 devices in a mesh: dp: 64 (over z, y, x_hi), tensor: 4 (over x_lo, core).
Axes of the slice: x: 4 (x_hi: 2, x_lo: 2; x = x_hi * 2 + x_lo), y: 4, z: 8, core: 2. Of those that a mesh axis runs over, the one named last changes fastest.
Arguments:
- final_input: bfloat16 [32768, 4096], P('dp'), may hold values from -20 to 20
- norm_gain: bfloat16 [4096], replicated, may hold values from 0.5 to 2
- value_weight: bfloat16 [4096, 1024], P(None, 'tensor'), may hold values from -0.09375 to 0.09375
- out_weight: bfloat16 [4096, 4096], P('tensor'), may hold values from -0.1875 to 0.1875
- cluster: int32 [32768, 1], P('dp'), may hold values from 0 to 255; in each aligned block of 512 rows (0 to 511, 512 to 1023, ...) at most 4 rows name the same one
- priority: int32 [32768], P('dp'), may hold values from 0 to 32767, each once
Outputs:
- best_match: float32 [32768], P('dp')
The draws below stay inside these ranges and needn't reach their ends.
Inputs may be any that keep to these rules, and one draw needn't show every extreme that they name: Among the rows of one device (aligned blocks of 512 documents), no cluster holds more than 4 documents, and some cluster holds exactly 4. `priority`: every rank appears exactly once.
All inputs are finite; a program needn't handle non-finite values.
Results may differ from the reference program's by a relative error of at most 0.0012.
Values may be sent and summed in bfloat16 or wider, within the bound.
No kernel may reach another device: no remote copies, remote signals or barrier semaphores. Data moves between devices by JAX's collectives and lax.ppermute only.
A program may use at most 128 MiB of HBM per device.

```python
import math
import jax
import jax.numpy as jnp
import numpy as np
from jax import lax

D = 4096
HEADS = 32
KV_HEADS = 8
HEAD_DIM = 128
DOC_DEV = 512
DOCS = 32768
CLUSTERS = 256
BUCKET = 4
N_DP = 64
N_TENSOR = 4


def draw_final_input(key, part):
    key = jax.random.fold_in(key, 7)
    keys = jax.random.split(key, 6)
    chosen = jax.random.randint(keys[0], (DOCS,), 0, 16)
    strength = jnp.exp(jax.random.uniform(keys[1], (DOCS, 1), jnp.float32, math.log(0.5), math.log(2.0)))
    row_scale = jnp.exp(jax.random.uniform(keys[2], (DOCS, 1), jnp.float32, math.log(0.3), math.log(3.0)))
    column_rough = jnp.exp(jax.random.uniform(keys[3], (1, D), jnp.float32, math.log(0.7), math.log(1.4)))
    position = jnp.arange(D, dtype=jnp.float32)[None, :] / D
    templates = jax.random.normal(keys[4], (16, D), jnp.float32)
    noise_part = jax.random.normal(keys[5], (DOCS, D), jnp.float32)
    column_ramp = 1.0 + 2.0 * position
    combined = strength * templates[chosen] + noise_part
    return jnp.clip(row_scale * column_ramp * column_rough * combined, -20.0, 20.0).astype(jnp.bfloat16)


def shard_levels(key, extent, pieces, low, top_value):
    gain = 1.0
    for dim, parts in pieces:
        heights = jax.random.uniform(jax.random.fold_in(jax.random.fold_in(key, 6), dim), (parts,), jnp.float32, low / len(pieces), top_value / len(pieces))
        gain = gain * jnp.repeat(jnp.exp(heights), extent[dim] // parts).reshape((-1,) + (1,) * (len(extent) - 1 - dim))
    return gain


def deal_out(rng, own, number, rows, count, top, limit, slope):
    order = jax.random.permutation(rng, count)
    packed, usual = load_shares(count, rows * top, limit, slope, True), load_shares(count, rows * top, limit, slope, False)
    places = jnp.arange(count)

    def named(lengths, turn):
        used = int((lengths > 0).sum())
        fixed = max(1, used // 4)
        passed = fixed + (places - fixed + turn * (used - fixed)) % max(1, count - fixed)
        return jnp.zeros((count,), jnp.int32).at[order[jnp.where(places < fixed, places, passed)]].set(jnp.asarray(lengths, jnp.int32))

    lengths = jnp.where(number % 4 == 0, named(packed, number // 4), named(usual, number - number // 4 - 1))
    mixed = jax.random.permutation(jax.random.fold_in(own, 3), count)
    giver, sink = mixed[0:count // 2 * 2:2], mixed[1:count // 2 * 2:2]
    room = jnp.minimum(lengths[giver] - 1, limit - lengths[sink]) // 2
    room = jnp.where((giver == order[0]) | (sink == order[0]) | (lengths[sink] == 0), 0, jnp.maximum(room, 0))
    passed = jax.random.randint(jax.random.fold_in(own, 4), (count // 2,), 0, 1 << 20) % (room + 1)
    lengths = lengths.at[giver].add(-passed).at[sink].add(passed)
    items = jnp.searchsorted(jnp.cumsum(lengths), jnp.arange(rows * top), side="right").astype(jnp.int32)
    listing = items.reshape(top, rows).T
    listing = listing[jax.random.permutation(jax.random.fold_in(own, 1), rows)]
    turn = jax.random.randint(jax.random.fold_in(own, 2), (rows, 1), 0, top)
    return jnp.take_along_axis(listing, (jnp.arange(top)[None, :] + turn) % top, axis=1)


def load_shares(count, total, bound, skew, full):
    loads = [(1 << 20) // math.isqrt(standing ** skew) + 1 for standing in range(1, count + 1)]
    largest = bound if full else min(bound, max(-(-total // count), total * loads[0] // sum(loads)))
    least = 1 if total - largest >= count - 1 else 0
    given, spare = [largest] + [least] * (count - 1), total - largest - least * (count - 1)
    while spare > 0:
        movable = [i for i in range(1, count) if given[i] < largest] or [i for i in range(1, count) if given[i] < bound]
        mass, budget = sum([loads[i] for i in movable]), spare
        for i in movable:
            extra = min(bound - given[i], max(1, budget * loads[i] // mass), spare)
            given[i] = given[i] + extra
            spare = spare - extra
    return np.array(given)


def scatter_about(key, shape, spread, limit, cuts=(), held_as=jnp.bfloat16):
    array = jax.random.normal(key, shape, jnp.float32) * spread
    if len(cuts) > 0:
        array = shard_levels(key, shape, cuts, -0.22, 0.18) * array
    return jnp.clip(array, min=-limit, max=limit).astype(held_as)


def setup_inputs(seed: int = 0) -> dict:
    seeds = jax.random.split(jax.random.key(seed), 7)
    final_input = draw_final_input(jax.random.fold_in(seeds[6], 71), 0)
    norm_gain = jnp.clip(jnp.exp(jax.random.uniform(seeds[1], (D,), jnp.float32, math.log(0.5), math.log(2.0))), 0.5, 2.0).astype(jnp.bfloat16)
    value_weight = scatter_about(seeds[2], (D, KV_HEADS * HEAD_DIM), D ** -0.5, 0.09375, ((1, 4),))
    out_weight = scatter_about(seeds[3], (HEADS * HEAD_DIM, D), (KV_HEADS * HEAD_DIM) ** -0.5, 0.1875, ((0, 4),))
    cluster_keys = jax.random.split(jax.random.fold_in(seeds[4], 1), DOCS // DOC_DEV)
    cluster_turns = jax.random.permutation(jax.random.fold_in(seeds[4], 3), DOCS // DOC_DEV)
    cluster = jax.vmap(lambda own, number: deal_out(jax.random.fold_in(seeds[4], 2), own, number, DOC_DEV, CLUSTERS, 1, BUCKET, 2))(cluster_keys, cluster_turns).reshape((DOCS, 1))
    priority = jax.random.permutation(seeds[5], DOCS).astype(jnp.int32)
    return {"final_input": final_input, "norm_gain": norm_gain, "value_weight": value_weight, "out_weight": out_weight, "cluster": cluster, "priority": priority}


def reference(final_input, norm_gain, value_weight, out_weight, cluster, priority):
    inputs_f32 = final_input.astype(jnp.float32)
    scaling = lax.rsqrt(lax.optimization_barrier(jnp.mean(inputs_f32 * inputs_f32, axis=1, keepdims=True)) + 1e-05)
    normed = (inputs_f32 * scaling * norm_gain.astype(jnp.float32)).astype(jnp.bfloat16)
    values = jnp.dot(normed, value_weight, preferred_element_type=jnp.float32).astype(jnp.bfloat16)
    group_size = HEADS // KV_HEADS
    attended = jnp.broadcast_to(values.reshape(DOCS, KV_HEADS, 1, HEAD_DIM), (DOCS, KV_HEADS, group_size, HEAD_DIM)).reshape(DOCS, HEADS * HEAD_DIM)
    block_width = HEADS * HEAD_DIM // N_TENSOR
    attention = jnp.zeros((DOCS, D), jnp.float32)
    for part_index in range(N_TENSOR):
        lower = part_index * block_width
        upper = lower + block_width
        term_block = jnp.dot(attended[:, lower:upper], out_weight[lower:upper], preferred_element_type=jnp.float32).astype(jnp.bfloat16)
        attention = attention + lax.optimization_barrier(term_block).astype(jnp.float32)
    hidden = inputs_f32 + attention
    squares = lax.optimization_barrier(jnp.sum(hidden * hidden, axis=1))
    embedded = hidden * lax.rsqrt(squares + 1e-06)[:, None]
    cluster_ids = cluster[:, 0].astype(jnp.int32)
    order = jnp.argsort(cluster_ids, stable=True).astype(jnp.int32)
    sorted_ids = cluster_ids[order]
    starts = jnp.searchsorted(sorted_ids, jnp.arange(CLUSTERS, dtype=jnp.int32)).astype(jnp.int32)
    within = jnp.arange(DOCS, dtype=jnp.int32) - starts[sorted_ids]
    capacity = N_DP * BUCKET
    table = jnp.full((CLUSTERS, capacity), -1, jnp.int32).at[sorted_ids, within].set(order)

    def one_cluster(members):
        present = members >= 0
        safe_index = jnp.where(present, members, 0)
        vectors = embedded[safe_index]
        ranking = jnp.where(present, priority[safe_index], DOCS)
        products = jnp.dot(vectors, vectors.T, precision=lax.Precision.HIGHEST, preferred_element_type=jnp.float32)
        allowed = (ranking[None, :] < ranking[:, None]) & present[None, :]
        highest = lax.optimization_barrier(jnp.max(jnp.where(allowed, products, -2.0), axis=1))
        return jnp.maximum(highest, -1.0)
    results = lax.map(one_cluster, table, batch_size=8)
    target = jnp.where(table >= 0, table, DOCS)
    return jnp.zeros((DOCS,), jnp.float32).at[target.reshape(-1)].set(results.reshape(-1), mode='drop')
```

```python
import jax
import jax.numpy as jnp
from jax import lax
from jax.experimental import pallas as pl
from jax.experimental.pallas import tpu as pltpu
from jax.sharding import PartitionSpec as P

HEADS = 32
KV_HEADS = 8
HEAD_DIM = 128
SLOTS = 4
LANES = 128
AXES = ("dp", "tensor")
F32 = jnp.float32
BF16 = jnp.bfloat16
MIB = 2**20
COLUMN_PARTS = 8
ROW_PARTS = 4
RANK_BASE = 128


def iota(shape, dim):
    return lax.broadcasted_iota(jnp.int32, shape, dim)


def chosen(flat_row, clusters, slot):
    rows = flat_row.shape[1]
    wanted = iota((clusters, rows), 0) * SLOTS + slot
    return flat_row == wanted


def blocks(width):
    return width // LANES


def pack_kernel(
    me_ref, cluster_ref, priority_ref, gain_ref, x_hbm, weight_hbm,
    flat_ref, message_hbm,
    x_ref, weight_ref, wide_ref, message_ref, select_ref, square_ref, in_sems, out_sems,
):
    rows, width = x_ref.shape
    clusters = select_ref.shape[1]
    depth = wide_ref.shape[0] // clusters
    me = me_ref[0]
    sentinel = me_ref[1]
    part = width // COLUMN_PARTS
    x_copies = []
    for j in range(COLUMN_PARTS):
        cols = pl.ds(j * part, part)
        copy = pltpu.make_async_copy(x_hbm.at[:, cols], x_ref.at[:, cols], in_sems.at[j])
        copy.start()
        x_copies.append(copy)
    weight_copy = pltpu.make_async_copy(weight_hbm, weight_ref, in_sems.at[COLUMN_PARTS])
    weight_copy.start()

    ids_row = cluster_ref[...]
    ids = jnp.transpose(jnp.broadcast_to(ids_row, (LANES, rows)))[:, 0:1]
    earlier = (ids == ids_row) & (iota((rows, rows), 0) < iota((rows, rows), 1))
    slot = jnp.sum(jnp.where(earlier, 1, 0), axis=0, keepdims=True)
    flat = ids_row * SLOTS + slot
    flat_ref[...] = jnp.broadcast_to(flat, flat_ref.shape)
    for s in range(SLOTS):
        select_ref[s] = jnp.where(chosen(flat, clusters, s), 1.0, 0.0).astype(BF16)

    def put(k, block):
        wide_ref[pl.ds(k, clusters, stride=depth), :] = block

    held = jnp.where(chosen(flat, clusters, me), priority_ref[...] - sentinel, 0)
    rank = jnp.sum(held, axis=1, keepdims=True) + sentinel
    rank = jnp.broadcast_to(rank, (clusters, LANES))
    put(depth - 2, (rank // RANK_BASE).astype(F32))
    put(depth - 1, (rank % RANK_BASE).astype(F32))

    mine = select_ref[me]
    square_ref[...] = jnp.zeros_like(square_ref)
    for j in range(COLUMN_PARTS):
        x_copies[j].wait()
        for k in range(j * part // LANES, (j + 1) * part // LANES, 2):
            picked = jnp.dot(mine, x_ref[:, k * LANES : (k + 2) * LANES], preferred_element_type=F32)
            put(k, picked[:, :LANES])
            put(k + 1, picked[:, LANES:])
        for r in range(0, rows, 128):
            total = square_ref[r : r + 128, :]
            for k in range(j * part // LANES, (j + 1) * part // LANES):
                block = x_ref[r : r + 128, k * LANES : (k + 1) * LANES].astype(F32)
                total = total + block * block
            square_ref[r : r + 128, :] = total

    gain = gain_ref[...].astype(F32)
    scale = lax.rsqrt(jnp.sum(square_ref[...], axis=1, keepdims=True) / width + 1e-05)
    for k in range(blocks(width)):
        cols = slice(k * LANES, (k + 1) * LANES)
        x_ref[:, cols] = (x_ref[:, cols].astype(F32) * scale * gain[k : k + 1, :]).astype(BF16)
    weight_copy.wait()
    values = jnp.dot(x_ref[...], weight_ref[...], preferred_element_type=F32).astype(BF16)
    pairs = blocks(weight_ref.shape[1])
    for s in range(SLOTS):
        picked = jnp.dot(select_ref[s], values, preferred_element_type=F32)
        for h in range(pairs):
            put(blocks(width) + s * pairs + h, picked[:, h * LANES : (h + 1) * LANES])

    share = wide_ref.shape[0] // ROW_PARTS
    out_copies = []
    for q in range(ROW_PARTS):
        span = pl.ds(q * share, share)
        message_ref[span, :] = wide_ref[span, :].astype(BF16)
        copy = pltpu.make_async_copy(message_ref.at[span, :], message_hbm.at[span, :], out_sems.at[q])
        copy.start()
        out_copies.append(copy)
    for copy in out_copies:
        copy.wait()


def pack(me, cluster, priority, gain, x, weight, clusters, depth):
    rows, width = x.shape
    vmem = pl.BlockSpec(memory_space=pltpu.VMEM)
    hbm = pl.BlockSpec(memory_space=pl.ANY)
    return pl.pallas_call(
        pack_kernel,
        in_specs=[pl.BlockSpec(memory_space=pltpu.SMEM), vmem, vmem, vmem, hbm, hbm],
        out_specs=[vmem, hbm],
        out_shape=[
            jax.ShapeDtypeStruct((8, rows), jnp.int32),
            jax.ShapeDtypeStruct((clusters * depth, LANES), BF16),
        ],
        scratch_shapes=[
            pltpu.VMEM((rows, width), BF16),
            pltpu.VMEM(weight.shape, BF16),
            pltpu.VMEM((clusters * depth, LANES), F32),
            pltpu.VMEM((clusters * depth, LANES), BF16),
            pltpu.VMEM((SLOTS, clusters, rows), BF16),
            pltpu.VMEM((rows, LANES), F32),
            pltpu.SemaphoreType.DMA((COLUMN_PARTS + 1,)),
            pltpu.SemaphoreType.DMA((ROW_PARTS,)),
        ],
        compiler_params=pltpu.CompilerParams(vmem_limit_bytes=56 * MIB),
        cost_estimate=pl.CostEstimate(
            flops=6 * clusters * rows * width, bytes_accessed=4 * rows * width, transcendentals=0
        ),
        name="pack",
    )(me, cluster, priority, gain, x, weight)


def owner_kernel(
    me_ref, got_hbm, w0, w1, w2a, w2b, w3a, w3b, out_ref,
    got_ref, wide_ref, weight_ref, mix_ref, value_ref, high, low, got_sems, weight_sems,
):
    clusters, width = high.shape
    depth = got_ref.shape[0] // clusters
    splits = SLOTS
    docs = clusters // splits
    kv_part = w0.shape[0]
    half = w2a.shape[0]
    pairs = blocks(kv_part)
    me = me_ref[0]
    share = got_ref.shape[0] // ROW_PARTS
    part = width // COLUMN_PARTS
    got_copies = []
    for q in range(ROW_PARTS):
        span = pl.ds(q * share, share)
        copy = pltpu.make_async_copy(got_hbm.at[span, :], got_ref.at[span, :], got_sems.at[q])
        copy.start()
        got_copies.append(copy)
    weight_copies = []
    for j in range(COLUMN_PARTS):
        cols = pl.ds(j * part, part)
        group = []
        for n, (source, other, shift) in enumerate(
            ((w0, 0, 0), (w1, 1, 0), (w2a, 2, 0), (w2b, 2, half), (w3a, 3, 0), (w3b, 3, half))
        ):
            start = pl.multiple_of((me ^ other) * kv_part + shift, half)
            copy = pltpu.make_async_copy(
                source.at[:, cols], weight_ref.at[pl.ds(start, source.shape[0]), cols], weight_sems.at[j, n]
            )
            copy.start()
            group.append(copy)
        weight_copies.append(group)

    for q in range(ROW_PARTS):
        span = pl.ds(q * share, share)
        got_copies[q].wait()
        wide_ref[span, :] = got_ref[span, :].astype(F32)
    for t in range(splits):
        for h in range(pairs):
            n = t * pairs + h
            for s in range(SLOTS):
                start = t * depth + blocks(width) + s * pairs + h
                piece = wide_ref[pl.ds(start, docs, stride=splits * depth), :]
                mix_ref[pl.ds(n * clusters + s, docs, stride=SLOTS), :] = piece
            value_ref[:, n * LANES : (n + 1) * LANES] = mix_ref[n * clusters : (n + 1) * clusters, :].astype(BF16)

    values = value_ref[...]
    for j in range(COLUMN_PARTS):
        for copy in weight_copies[j]:
            copy.wait()
        for k in range(j * part // LANES, (j + 1) * part // LANES, 2):
            cols = slice(k * LANES, (k + 2) * LANES)
            left = wide_ref[pl.ds(k, clusters, stride=depth), :]
            right = wide_ref[pl.ds(k + 1, clusters, stride=depth), :]
            hidden = jnp.concatenate([left, right], axis=1) + jnp.dot(
                values, weight_ref[:, cols], preferred_element_type=F32
            )
            upper = hidden.astype(BF16)
            high[:, cols] = upper
            low[:, cols] = (hidden - upper.astype(F32)).astype(BF16)
    contract = (((1,), (1,)), ((), ()))
    gram = lax.dot_general(high[...], high[...], contract, preferred_element_type=F32)
    cross = lax.dot_general(high[...], low[...], contract, preferred_element_type=F32)

    total = gram + (cross + jnp.transpose(cross))
    size = (clusters, clusters)
    diagonal = jnp.where(iota(size, 0) == iota(size, 1), total, 0.0)
    inv_col = lax.rsqrt(jnp.sum(diagonal, axis=1, keepdims=True) + 1e-06)
    inv_row = lax.rsqrt(jnp.sum(diagonal, axis=0, keepdims=True) + 1e-06)
    similarity = total * inv_col * inv_row
    rank = wide_ref[pl.ds(depth - 2, clusters, stride=depth), :] * RANK_BASE
    rank = rank + wide_ref[pl.ds(depth - 1, clusters, stride=depth), :]
    rank_row = jnp.transpose(rank)[0:1, :]
    allowed = rank[:, 0:1] < rank_row
    best = jnp.max(jnp.where(allowed, similarity, -2.0), axis=0, keepdims=True)
    best = jnp.maximum(best, -1.0)
    lane = iota(out_ref.shape, 1)
    result = jnp.zeros(out_ref.shape, F32)
    for s in range(SLOTS):
        wanted = (iota(size, 0) // SLOTS) * SLOTS + s
        mine = jnp.max(jnp.where(iota(size, 1) == wanted, best, -4.0), axis=1, keepdims=True)
        result = jnp.where(lane == s, mine, result)
    out_ref[...] = result


def owner_best(me, got, weights, clusters, width):
    depth = got.shape[0] // clusters
    kv_width = SLOTS * weights[0].shape[0]
    hbm = pl.BlockSpec(memory_space=pl.ANY)
    return pl.pallas_call(
        owner_kernel,
        in_specs=[pl.BlockSpec(memory_space=pltpu.SMEM), hbm] + [hbm] * len(weights),
        out_specs=pl.BlockSpec(memory_space=pltpu.VMEM),
        out_shape=jax.ShapeDtypeStruct((clusters, LANES), F32),
        scratch_shapes=[
            pltpu.VMEM(got.shape, BF16),
            pltpu.VMEM(got.shape, F32),
            pltpu.VMEM((kv_width, width), BF16),
            pltpu.VMEM((kv_width // LANES * clusters, LANES), F32),
            pltpu.VMEM((clusters, kv_width), BF16),
            pltpu.VMEM((clusters, width), BF16),
            pltpu.VMEM((clusters, width), BF16),
            pltpu.SemaphoreType.DMA((ROW_PARTS,)),
            pltpu.SemaphoreType.DMA((COLUMN_PARTS, len(weights))),
        ],
        compiler_params=pltpu.CompilerParams(vmem_limit_bytes=56 * MIB),
        cost_estimate=pl.CostEstimate(
            flops=4 * clusters * kv_width * width, bytes_accessed=12 * MIB, transcendentals=0
        ),
        name="owner_best",
    )(me, got, *weights)


def pick_kernel(flat_ref, best_ref, out_ref):
    clusters = best_ref.shape[0]
    flat = flat_ref[0:1, :]
    result = jnp.zeros((1, flat.shape[1]), F32)
    for s in range(SLOTS):
        held = jnp.where(chosen(flat, clusters, s), best_ref[:, s : s + 1], 0.0)
        result = result + jnp.sum(held, axis=0, keepdims=True)
    out_ref[...] = result


def pick(flat, best):
    vmem = pl.BlockSpec(memory_space=pltpu.VMEM)
    return pl.pallas_call(
        pick_kernel,
        in_specs=[vmem, vmem],
        out_specs=vmem,
        out_shape=jax.ShapeDtypeStruct((1, flat.shape[1]), F32),
        name="pick",
    )(flat, best)


def ring_pairs(splits, owners, way):
    cores = 2
    low = splits // cores
    length = 2 * low
    pairs = []
    for d in range(owners):
        for t in range(splits):
            x = (d % 2) * low + t // cores
            to = (x + way) % length
            other = (d // 2 * 2 + to // low) * splits + (to % low) * cores + t % cores
            pairs.append((d * splits + t, other))
    return pairs


def spread_weights(folded, splits, owners):
    half = folded.shape[0] // 2
    swap = [(t, t ^ 1) for t in range(splits)]
    first = lax.ppermute(folded[:half], AXES, ring_pairs(splits, owners, 1))
    second = lax.ppermute(folded[half:], AXES, ring_pairs(splits, owners, -1))
    beside = lax.ppermute(folded, "tensor", swap)
    return [folded, beside, first, second, lax.ppermute(first, "tensor", swap), lax.ppermute(second, "tensor", swap)]


def shards(final_input, norm_gain, value_weight, out_weight, cluster, priority):
    rows, width = final_input.shape
    splits = lax.axis_size("tensor")
    owners = lax.axis_size("dp")
    clusters = splits * owners
    me = jnp.stack([lax.axis_index("tensor").astype(jnp.int32), jnp.int32(owners * rows)])
    depth = blocks(width) + SLOTS * blocks(value_weight.shape[1]) + 2
    flat, message = pack(
        me,
        cluster.reshape(1, rows),
        priority.reshape(1, rows),
        norm_gain.reshape(blocks(width), LANES),
        final_input,
        value_weight,
        clusters,
        depth,
    )
    got = lax.all_to_all(message.reshape(clusters, depth // 2, 2, LANES), AXES, 0, 0, tiled=True)
    got = got.reshape(clusters * depth, LANES)
    kv_local = value_weight.shape[1] // HEAD_DIM
    group = HEADS // KV_HEADS
    out_weight, _ = lax.optimization_barrier((out_weight, flat))
    folded = jnp.sum(out_weight.reshape(kv_local, group, HEAD_DIM, width).astype(F32), axis=1)
    folded = folded.reshape(kv_local * HEAD_DIM, width).astype(BF16)
    weights = spread_weights(folded, splits, owners)
    best = owner_best(me, got, weights, clusters, width)
    returned = lax.all_to_all(best, AXES, 0, 0, tiled=True)
    return pick(flat, returned).reshape(rows)


def solution(mesh):
    in_specs = (P("dp", None), P(), P(None, "tensor"), P("tensor", None), P("dp", None), P("dp"))
    return jax.shard_map(shards, mesh=mesh, in_specs=in_specs, out_specs=P("dp"), check_vma=False)
```

```python
import functools

import jax
import jax.numpy as jnp
from jax import lax
from jax.experimental import pallas as pl
from jax.experimental.pallas import tpu as pltpu
from jax.sharding import PartitionSpec as P

HEADS = 32
KV_HEADS = 8
HEAD_DIM = 128
SLOTS = 4
LANES = 128
AXES = ("dp", "tensor")
F32 = jnp.float32
BF16 = jnp.bfloat16
MIB = 2**20
COLUMN_PARTS = 2
ROW_PARTS = 4
OWNER_PARTS = 4
RANK_BASE = 128


def iota(shape, dim):
    return lax.broadcasted_iota(jnp.int32, shape, dim)


def chosen(flat_row, clusters, slot):
    rows = flat_row.shape[1]
    wanted = iota((clusters, rows), 0) * SLOTS + slot
    return flat_row == wanted


def blocks(width):
    return width // LANES


def pack_kernel(
    sentinel, cluster_ref, priority_ref, gain_ref, x_hbm, weight_hbm,
    flat_ref, message_ref,
    x_ref, weight_ref, scaled_ref, wide_ref, select_ref, square_ref, product_ref, in_sems,
):
    rows, width = x_ref.shape
    clusters = select_ref.shape[1]
    depth = wide_ref.shape[0] // clusters
    part = width // COLUMN_PARTS
    weight_copy = pltpu.make_async_copy(weight_hbm, weight_ref, in_sems.at[COLUMN_PARTS])
    weight_copy.start()
    x_copies = []
    for j in range(COLUMN_PARTS):
        cols = pl.ds(j * part, part)
        copy = pltpu.make_async_copy(x_hbm.at[:, cols], x_ref.at[:, cols], in_sems.at[j])
        copy.start()
        x_copies.append(copy)

    me = lax.axis_index("tensor").astype(jnp.int32)
    ids_row = cluster_ref[...]
    ids = jnp.transpose(jnp.broadcast_to(ids_row, (LANES, rows)))[:, 0:1]
    earlier = (ids == ids_row) & (iota((rows, rows), 0) < iota((rows, rows), 1))
    slot = jnp.sum(jnp.where(earlier, 1, 0), axis=0, keepdims=True)
    flat = ids_row * SLOTS + slot
    flat_ref[...] = jnp.broadcast_to(flat, flat_ref.shape)
    for s in range(SLOTS):
        select_ref[s] = jnp.where(chosen(flat, clusters, s), 1.0, 0.0).astype(BF16)

    def put(k, block):
        wide_ref[pl.ds(k, clusters, stride=depth), :] = block

    held = jnp.where(chosen(flat, clusters, me), priority_ref[...] - sentinel, 0)
    rank = jnp.sum(held, axis=1, keepdims=True) + sentinel
    rank = jnp.broadcast_to(rank, (clusters, LANES))
    put(depth - 2, (rank // RANK_BASE).astype(F32))
    put(depth - 1, (rank % RANK_BASE).astype(F32))

    weight_copy.wait()
    gain = jnp.transpose(gain_ref[...].astype(F32))
    for k in range(blocks(width)):
        span = slice(k * LANES, (k + 1) * LANES)
        scaled_ref[span, :] = (weight_ref[span, :].astype(F32) * gain[:, k : k + 1]).astype(BF16)

    mine = select_ref[me]
    square_ref[...] = jnp.zeros_like(square_ref)
    product_ref[...] = jnp.zeros_like(product_ref)
    for j in range(COLUMN_PARTS):
        x_copies[j].wait()
        for k in range(j * part // LANES, (j + 1) * part // LANES, 2):
            picked = jnp.dot(mine, x_ref[:, k * LANES : (k + 2) * LANES], preferred_element_type=F32)
            put(k, picked[:, :LANES])
            put(k + 1, picked[:, LANES:])
        span = slice(j * part, (j + 1) * part)
        product_ref[...] += jnp.dot(x_ref[:, span], scaled_ref[span, :], preferred_element_type=F32)
        for r in range(0, rows, 128):
            total = square_ref[r : r + 128, :]
            for k in range(j * part // LANES, (j + 1) * part // LANES):
                block = x_ref[r : r + 128, k * LANES : (k + 1) * LANES].astype(F32)
                total = total + block * block
            square_ref[r : r + 128, :] = total

    scale = lax.rsqrt(jnp.sum(square_ref[...], axis=1, keepdims=True) / width + 1e-05)
    values = (product_ref[...] * scale).astype(BF16)
    pairs = blocks(weight_ref.shape[1])
    for s in range(SLOTS):
        picked = jnp.dot(select_ref[s], values, preferred_element_type=F32)
        for h in range(pairs):
            put(blocks(width) + s * pairs + h, picked[:, h * LANES : (h + 1) * LANES])

    share = wide_ref.shape[0] // ROW_PARTS
    for q in range(ROW_PARTS):
        span = pl.ds(q * share, share)
        message_ref[span, :] = wide_ref[span, :].astype(BF16)


def pack(cluster, priority, gain, x, weight, clusters, depth, sentinel):
    rows, width = x.shape
    vmem = pl.BlockSpec(memory_space=pltpu.VMEM)
    hbm = pl.BlockSpec(memory_space=pl.ANY)
    return pl.pallas_call(
        functools.partial(pack_kernel, sentinel),
        in_specs=[vmem, vmem, vmem, hbm, hbm],
        out_specs=[vmem, vmem],
        out_shape=[
            jax.ShapeDtypeStruct((8, rows), jnp.int32),
            pltpu.VMEM((clusters * depth, LANES), BF16),
        ],
        scratch_shapes=[
            pltpu.VMEM((rows, width), BF16),
            pltpu.VMEM(weight.shape, BF16),
            pltpu.VMEM(weight.shape, BF16),
            pltpu.VMEM((clusters * depth, LANES), F32),
            pltpu.VMEM((SLOTS, clusters, rows), BF16),
            pltpu.VMEM((rows, LANES), F32),
            pltpu.VMEM((rows, weight.shape[1]), F32),
            pltpu.SemaphoreType.DMA((COLUMN_PARTS + 1,)),
        ],
        compiler_params=pltpu.CompilerParams(vmem_limit_bytes=58 * MIB),
        cost_estimate=pl.CostEstimate(
            flops=6 * clusters * rows * width, bytes_accessed=4 * rows * width, transcendentals=0
        ),
        name="pack",
    )(cluster, priority, gain, x, weight)


def owner_kernel(
    got_hbm, w0, w1, w2, w3, out_ref,
    got_ref, wide_ref, weight_ref, mix_ref, value_ref, high, low, gram_ref, cross_ref, got_sems, weight_sems,
):
    clusters, width = high.shape
    depth = got_ref.shape[0] // clusters
    splits = SLOTS
    docs = clusters // splits
    kv_part = w0.shape[0]
    pairs = blocks(kv_part)
    share = got_ref.shape[0] // ROW_PARTS
    got_copies = []
    for q in range(ROW_PARTS):
        span = pl.ds(q * share, share)
        copy = pltpu.make_async_copy(got_hbm.at[span, :], got_ref.at[span, :], got_sems.at[q])
        copy.start()
        got_copies.append(copy)
    me = lax.axis_index("tensor").astype(jnp.int32)
    part = width // OWNER_PARTS
    weight_copies = []
    for j in range(OWNER_PARTS):
        cols = pl.ds(j * part, part)
        group = []
        for n, source in enumerate((w0, w1, w2, w3)):
            start = pl.multiple_of((me ^ n) * kv_part, kv_part)
            group.append(
                pltpu.make_async_copy(
                    source.at[:, cols], weight_ref.at[pl.ds(start, kv_part), cols], weight_sems.at[j, n]
                )
            )
        weight_copies.append(group)

    def start_weights(j):
        for copy in weight_copies[j]:
            copy.start()

    start_weights(0)
    for q in range(ROW_PARTS):
        span = pl.ds(q * share, share)
        got_copies[q].wait()
        wide_ref[span, :] = got_ref[span, :].astype(F32)
    for j in range(1, OWNER_PARTS):
        start_weights(j)
    for t in range(splits):
        for h in range(pairs):
            n = t * pairs + h
            for s in range(SLOTS):
                start = t * depth + blocks(width) + s * pairs + h
                piece = wide_ref[pl.ds(start, docs, stride=splits * depth), :]
                mix_ref[pl.ds(n * clusters + s, docs, stride=SLOTS), :] = piece
            value_ref[:, n * LANES : (n + 1) * LANES] = mix_ref[n * clusters : (n + 1) * clusters, :].astype(BF16)

    values = value_ref[...]
    contract = (((1,), (1,)), ((), ()))
    for j in range(OWNER_PARTS):
        for copy in weight_copies[j]:
            copy.wait()
        for k in range(j * part // LANES, (j + 1) * part // LANES, 2):
            cols = slice(k * LANES, (k + 2) * LANES)
            left = wide_ref[pl.ds(k, clusters, stride=depth), :]
            right = wide_ref[pl.ds(k + 1, clusters, stride=depth), :]
            hidden = jnp.concatenate([left, right], axis=1) + jnp.dot(
                values, weight_ref[:, cols], preferred_element_type=F32
            )
            upper = hidden.astype(BF16)
            high[:, cols] = upper
            low[:, cols] = (hidden - upper.astype(F32)).astype(BF16)
        cols = slice(j * part, (j + 1) * part)
        gram = lax.dot_general(high[:, cols], high[:, cols], contract, preferred_element_type=F32)
        cross = lax.dot_general(high[:, cols], low[:, cols], contract, preferred_element_type=F32)
        gram_ref[...] = gram if j == 0 else gram_ref[...] + gram
        cross_ref[...] = cross if j == 0 else cross_ref[...] + cross

    gram = gram_ref[...]
    cross = cross_ref[...]
    total = gram + (cross + jnp.transpose(cross))
    size = (clusters, clusters)
    diagonal = jnp.where(iota(size, 0) == iota(size, 1), total, 0.0)
    inv_col = lax.rsqrt(jnp.sum(diagonal, axis=1, keepdims=True) + 1e-06)
    inv_row = lax.rsqrt(jnp.sum(diagonal, axis=0, keepdims=True) + 1e-06)
    similarity = total * inv_col * inv_row
    rank = wide_ref[pl.ds(depth - 2, clusters, stride=depth), :] * RANK_BASE
    rank = rank + wide_ref[pl.ds(depth - 1, clusters, stride=depth), :]
    rank_row = jnp.transpose(rank)[0:1, :]
    allowed = rank[:, 0:1] < rank_row
    best = jnp.max(jnp.where(allowed, similarity, -2.0), axis=0, keepdims=True)
    best = jnp.maximum(best, -1.0)
    lane = iota(out_ref.shape, 1)
    result = jnp.zeros(out_ref.shape, F32)
    for s in range(SLOTS):
        wanted = (iota(size, 0) // SLOTS) * SLOTS + s
        mine = jnp.max(jnp.where(iota(size, 1) == wanted, best, -4.0), axis=1, keepdims=True)
        result = jnp.where(lane == s, mine, result)
    out_ref[...] = result


def owner_best(got, weights, clusters):
    kv_part, width = weights[0].shape
    height = kv_part * len(weights)
    hbm = pl.BlockSpec(memory_space=pl.ANY)
    return pl.pallas_call(
        owner_kernel,
        in_specs=[hbm] * (1 + len(weights)),
        out_specs=pl.BlockSpec(memory_space=pltpu.VMEM),
        out_shape=jax.ShapeDtypeStruct((clusters, LANES), F32),
        scratch_shapes=[
            pltpu.VMEM(got.shape, BF16),
            pltpu.VMEM(got.shape, F32),
            pltpu.VMEM((height, width), BF16),
            pltpu.VMEM((height // LANES * clusters, LANES), F32),
            pltpu.VMEM((clusters, height), BF16),
            pltpu.VMEM((clusters, width), BF16),
            pltpu.VMEM((clusters, width), BF16),
            pltpu.VMEM((clusters, clusters), F32),
            pltpu.VMEM((clusters, clusters), F32),
            pltpu.SemaphoreType.DMA((ROW_PARTS,)),
            pltpu.SemaphoreType.DMA((OWNER_PARTS, len(weights))),
        ],
        compiler_params=pltpu.CompilerParams(vmem_limit_bytes=58 * MIB),
        cost_estimate=pl.CostEstimate(
            flops=4 * clusters * height * width, bytes_accessed=12 * MIB, transcendentals=0
        ),
        name="owner_best",
    )(got, *weights)


def pick_kernel(flat_ref, best_ref, out_ref):
    clusters = best_ref.shape[0]
    flat = flat_ref[0:1, :]
    result = jnp.zeros((1, flat.shape[1]), F32)
    for s in range(SLOTS):
        held = jnp.where(chosen(flat, clusters, s), best_ref[:, s : s + 1], 0.0)
        result = result + jnp.sum(held, axis=0, keepdims=True)
    out_ref[...] = result


def pick(flat, best):
    vmem = pl.BlockSpec(memory_space=pltpu.VMEM)
    return pl.pallas_call(
        pick_kernel,
        in_specs=[vmem, vmem],
        out_specs=vmem,
        out_shape=jax.ShapeDtypeStruct((1, flat.shape[1]), F32),
        name="pick",
    )(flat, best)


def ring_pairs(splits, owners):
    cores = 2
    low = splits // cores
    length = 2 * low
    pairs = []
    for d in range(owners):
        for t in range(splits):
            x = (d % 2) * low + t // cores
            to = (x + (1 if t % cores == 0 else -1)) % length
            other = (d // 2 * 2 + to // low) * splits + (to % low) * cores + t % cores
            pairs.append((d * splits + t, other))
    return pairs


def spread(part, splits, owners):
    swap = [(t, t ^ 1) for t in range(splits)]
    across = lax.ppermute(part, AXES, ring_pairs(splits, owners))
    return [part, lax.ppermute(part, "tensor", swap), across, lax.ppermute(across, "tensor", swap)]


def shards(final_input, norm_gain, value_weight, out_weight, cluster, priority):
    rows, width = final_input.shape
    splits = lax.axis_size("tensor")
    owners = lax.axis_size("dp")
    clusters = splits * owners
    depth = blocks(width) + SLOTS * blocks(value_weight.shape[1]) + 2
    flat, message = pack(
        cluster.reshape(1, rows),
        priority.reshape(1, rows),
        norm_gain.reshape(blocks(width), LANES),
        final_input,
        value_weight,
        clusters,
        depth,
        owners * rows,
    )
    got = lax.all_to_all(message.reshape(clusters, depth // 2, 2, LANES), AXES, 0, 0, tiled=True)
    got = got.reshape(clusters * depth, LANES)
    kv_local = value_weight.shape[1] // HEAD_DIM
    group = HEADS // KV_HEADS
    out_weight, _ = lax.optimization_barrier((out_weight, flat))
    folded = jnp.sum(out_weight.reshape(kv_local, group, HEAD_DIM, width).astype(F32), axis=1)
    folded = folded.reshape(kv_local * HEAD_DIM, width).astype(BF16)
    weights = spread(folded, splits, owners)
    best = owner_best(got, weights, clusters)
    returned = lax.all_to_all(best, AXES, 0, 0, tiled=True)
    return pick(flat, returned).reshape(rows)


def solution(mesh):
    in_specs = (P("dp", None), P(), P(None, "tensor"), P("tensor", None), P("dp", None), P("dp"))
    return jax.shard_map(shards, mesh=mesh, in_specs=in_specs, out_specs=P("dp"), check_vma=False)
```

```python
import functools

import jax
import jax.numpy as jnp
from jax import lax
from jax.experimental import pallas as pl
from jax.experimental.pallas import tpu as pltpu
from jax.sharding import PartitionSpec as P

HEADS = 32
KV_HEADS = 8
HEAD_DIM = 128
SLOTS = 4
LANES = 128
AXES = ("dp", "tensor")
F32 = jnp.float32
BF16 = jnp.bfloat16
MIB = 2**20
COLUMN_PARTS = 2
ROW_PARTS = 4
OWNER_PARTS = 4
PROJECT_PARTS = 4
AHEAD = 3
FOLD_PARTS = 8
RANK_BASE = 128


def iota(shape, dim):
    return lax.broadcasted_iota(jnp.int32, shape, dim)


def chosen(flat_row, clusters, slot):
    rows = flat_row.shape[1]
    wanted = iota((clusters, rows), 0) * SLOTS + slot
    return flat_row == wanted


def blocks(width):
    return width // LANES


def row_parity():
    return (lax.axis_index("dp").astype(jnp.int32) // 2) % 2


def pack_kernel(
    sentinel, cluster_ref, priority_ref, x_hbm, project_hbm, flat_ref, message_ref, half_hbm, x_ref, wide_ref, half_ref, sems,
):
    rows, width = x_ref.shape
    part = width // COLUMN_PARTS
    x_copies = []
    for j in range(COLUMN_PARTS):
        cols = pl.ds(j * part, part)
        copy = pltpu.make_async_copy(x_hbm.at[:, cols], x_ref.at[:, cols], sems.at[j])
        copy.start()
        x_copies.append(copy)
    half = half_hbm.shape[0]
    start = pl.multiple_of(row_parity() * half, half)
    half_in = pltpu.make_async_copy(project_hbm.at[pl.ds(start, half), :], half_ref, sems.at[COLUMN_PARTS])
    half_in.start()

    me = lax.axis_index("tensor").astype(jnp.int32)
    ids_row = cluster_ref[...]
    ids = jnp.transpose(jnp.broadcast_to(ids_row, (LANES, rows)))[:, 0:1]
    earlier = (ids == ids_row) & (iota((rows, rows), 0) < iota((rows, rows), 1))
    slot = jnp.sum(jnp.where(earlier, 1, 0), axis=0, keepdims=True)
    flat = ids_row * SLOTS + slot
    flat_ref[...] = jnp.broadcast_to(flat, flat_ref.shape)
    depth = blocks(width) + 2
    clusters = wide_ref.shape[0] // depth

    def put(k, block):
        wide_ref[pl.ds(k, clusters, stride=depth), :] = block

    mine = chosen(flat, clusters, me)
    held = jnp.where(mine, priority_ref[...] - sentinel, 0)
    rank = jnp.sum(held, axis=1, keepdims=True) + sentinel
    rank = jnp.broadcast_to(rank, (clusters, LANES))
    put(depth - 2, (rank // RANK_BASE).astype(F32))
    put(depth - 1, (rank % RANK_BASE).astype(F32))

    select = jnp.where(mine, 1.0, 0.0).astype(BF16)
    half_out = pltpu.make_async_copy(half_ref, half_hbm, sems.at[COLUMN_PARTS + 1])
    for j in range(COLUMN_PARTS):
        x_copies[j].wait()
        if j == COLUMN_PARTS - 1:
            half_in.wait()
            half_out.start()
        for k in range(j * part // LANES, (j + 1) * part // LANES, 2):
            picked = jnp.dot(select, x_ref[:, k * LANES : (k + 2) * LANES], preferred_element_type=F32)
            put(k, picked[:, :LANES])
            put(k + 1, picked[:, LANES:])

    share = wide_ref.shape[0] // ROW_PARTS
    for q in range(ROW_PARTS):
        span = pl.ds(q * share, share)
        message_ref[span, :] = wide_ref[span, :].astype(BF16)
    half_out.wait()


def pack(cluster, priority, x, project, clusters, depth, sentinel):
    rows, width = x.shape
    hbm = pl.BlockSpec(memory_space=pl.ANY)
    vmem = pl.BlockSpec(memory_space=pltpu.VMEM)
    return pl.pallas_call(
        functools.partial(pack_kernel, sentinel),
        in_specs=[vmem, vmem, hbm, hbm],
        out_specs=[vmem, vmem, hbm],
        out_shape=[
            jax.ShapeDtypeStruct((8, rows), jnp.int32),
            pltpu.VMEM((clusters * depth, LANES), BF16),
            jax.ShapeDtypeStruct((project.shape[0] // 2, project.shape[1]), BF16),
        ],
        scratch_shapes=[
            pltpu.VMEM((rows, width), BF16),
            pltpu.VMEM((clusters * depth, LANES), F32),
            pltpu.VMEM((project.shape[0] // 2, project.shape[1]), BF16),
            pltpu.SemaphoreType.DMA((COLUMN_PARTS + 2,)),
        ],
        compiler_params=pltpu.CompilerParams(vmem_limit_bytes=58 * MIB),
        cost_estimate=pl.CostEstimate(
            flops=2 * clusters * rows * width, bytes_accessed=3 * rows * width, transcendentals=0
        ),
        name="pack",
    )(cluster, priority, x, project)


def fold_kernel(weight_hbm, out_hbm, half_hbm, weight_ref, out_ref, in_sems, out_sems, half_sem):
    group = HEADS // KV_HEADS
    kv_part, width = out_ref.shape
    part = width // FOLD_PARTS
    in_copies = []
    for j in range(FOLD_PARTS):
        cols = pl.ds(j * part, part)
        copy = pltpu.make_async_copy(weight_hbm.at[:, cols], weight_ref.at[:, cols], in_sems.at[j])
        copy.start()
        in_copies.append(copy)
    out_copies = []
    for j in range(FOLD_PARTS):
        in_copies[j].wait()
        cols = slice(j * part, (j + 1) * part)
        for kv in range(kv_part // HEAD_DIM):
            total = 0.0
            for g in range(group):
                start = (kv * group + g) * HEAD_DIM
                total = total + weight_ref[start : start + HEAD_DIM, cols].astype(F32)
            out_ref[kv * HEAD_DIM : (kv + 1) * HEAD_DIM, cols] = total.astype(BF16)
        span = pl.ds(j * part, part)
        copy = pltpu.make_async_copy(out_ref.at[:, span], out_hbm.at[:, span], out_sems.at[j])
        copy.start()
        out_copies.append(copy)
    half = half_hbm.shape[0]
    start = pl.multiple_of(row_parity() * half, half)
    copy = pltpu.make_async_copy(out_ref.at[pl.ds(start, half), :], half_hbm, half_sem)
    copy.start()
    out_copies.append(copy)
    for copy in out_copies:
        copy.wait()


def fold(out_weight):
    height, width = out_weight.shape
    kv_part = height * KV_HEADS // HEADS
    hbm = pl.BlockSpec(memory_space=pl.ANY)
    return pl.pallas_call(
        fold_kernel,
        in_specs=[hbm],
        out_specs=[hbm, hbm],
        out_shape=[
            jax.ShapeDtypeStruct((kv_part, width), BF16),
            jax.ShapeDtypeStruct((kv_part // 2, width), BF16),
        ],
        scratch_shapes=[
            pltpu.VMEM(out_weight.shape, BF16),
            pltpu.VMEM((kv_part, width), BF16),
            pltpu.SemaphoreType.DMA((FOLD_PARTS,)),
            pltpu.SemaphoreType.DMA((FOLD_PARTS,)),
            pltpu.SemaphoreType.DMA,
        ],
        compiler_params=pltpu.CompilerParams(vmem_limit_bytes=58 * MIB),
        cost_estimate=pl.CostEstimate(flops=4 * 10**11, bytes_accessed=10 * MIB, transcendentals=0),
        name="fold",
    )(out_weight)


def owner_kernel(
    gain_ref, got_hbm, v0, v1, v2, v2y, v3, v3y, w0, w1, w2, w2y, w3, w3y, out_ref,
    got_ref, wide_ref, x_ref, gained_ref, project_ref, weight_ref, high, low, gram_ref, cross_ref, product_ref,
    got_sems, project_sems, weight_sems,
):
    clusters, width = high.shape
    depth = got_ref.shape[0] // clusters
    kv_part = w0.shape[0]
    share = got_ref.shape[0] // ROW_PARTS
    got_copies = []
    for q in range(ROW_PARTS):
        span = pl.ds(q * share, share)
        got_copies.append(pltpu.make_async_copy(got_hbm.at[span, :], got_ref.at[span, :], got_sems.at[q]))
    half = v2.shape[0]
    near = row_parity() * half
    far = half - near
    step = 2 * half // PROJECT_PARTS
    starts = []
    project_groups = []
    for p in range(PROJECT_PARTS):
        inner = p * step % half
        begin = pl.multiple_of((near if p * step < half else far) + inner, step)
        starts.append(begin)
        third, fourth = (v2, v3) if p * step < half else (v2y, v3y)
        project_groups.append(
            [
                pltpu.make_async_copy(
                    source.at[pl.ds(first, step), :],
                    project_ref.at[p, :, pl.ds(n * kv_part, kv_part)],
                    project_sems.at[p, n],
                )
                for n, (source, first) in enumerate(((v0, begin), (v1, begin), (third, inner), (fourth, inner)))
            ]
        )
    part = width // OWNER_PARTS
    rows = w2.shape[0]
    near = row_parity() * rows
    far = rows - near
    weight_groups = []
    for j in range(OWNER_PARTS):
        cols = pl.ds(j * part, part)
        group = []
        for i, (source, n, shift) in enumerate(
            ((w0, 0, 0), (w1, 1, 0), (w2, 2, near), (w2y, 2, far), (w3, 3, near), (w3y, 3, far))
        ):
            span = pl.ds(pl.multiple_of(n * kv_part + shift, rows), source.shape[0])
            group.append(
                pltpu.make_async_copy(source.at[:, cols], weight_ref.at[span, cols], weight_sems.at[j, i])
            )
        weight_groups.append(group)
    groups = project_groups + weight_groups

    def start(n):
        if n < len(groups):
            for copy in groups[n]:
                copy.start()

    for copy in got_copies:
        copy.start()
    for q in range(ROW_PARTS):
        span = pl.ds(q * share, share)
        got_copies[q].wait()
        if q >= ROW_PARTS - AHEAD:
            start(q - ROW_PARTS + AHEAD)
        wide_ref[span, :] = got_ref[span, :].astype(F32)
    gain = gain_ref[...].astype(F32)
    squares = jnp.zeros((clusters, LANES), F32)
    for k in range(blocks(width)):
        cols = slice(k * LANES, (k + 1) * LANES)
        block = wide_ref[pl.ds(k, clusters, stride=depth), :]
        squares = squares + block * block
        x_ref[:, cols] = block.astype(BF16)
        gained_ref[:, cols] = (block * gain[k : k + 1, :]).astype(BF16)
    for p in range(PROJECT_PARTS):
        for copy in project_groups[p]:
            copy.wait()
        start(p + AHEAD)
        product = jnp.dot(
            gained_ref[:, pl.ds(starts[p], step)], project_ref[p], preferred_element_type=F32
        )
        product_ref[...] = product if p == 0 else product_ref[...] + product
    scale = lax.rsqrt(jnp.sum(squares, axis=1, keepdims=True) / width + 1e-05)
    values = (product_ref[...] * scale).astype(BF16)
    contract = (((1,), (1,)), ((), ()))
    for j in range(OWNER_PARTS):
        for copy in weight_groups[j]:
            copy.wait()
        start(PROJECT_PARTS + j + AHEAD)
        for k in range(j * part // LANES, (j + 1) * part // LANES, 2):
            cols = slice(k * LANES, (k + 2) * LANES)
            hidden = x_ref[:, cols].astype(F32) + jnp.dot(
                values, weight_ref[:, cols], preferred_element_type=F32
            )
            upper = hidden.astype(BF16)
            high[:, cols] = upper
            low[:, cols] = (hidden - upper.astype(F32)).astype(BF16)
        cols = slice(j * part, (j + 1) * part)
        gram = lax.dot_general(high[:, cols], high[:, cols], contract, preferred_element_type=F32)
        cross = lax.dot_general(high[:, cols], low[:, cols], contract, preferred_element_type=F32)
        gram_ref[...] = gram if j == 0 else gram_ref[...] + gram
        cross_ref[...] = cross if j == 0 else cross_ref[...] + cross

    gram = gram_ref[...]
    cross = cross_ref[...]
    total = gram + (cross + jnp.transpose(cross))
    size = (clusters, clusters)
    diagonal = jnp.where(iota(size, 0) == iota(size, 1), total, 0.0)
    inv_col = lax.rsqrt(jnp.sum(diagonal, axis=1, keepdims=True) + 1e-06)
    inv_row = lax.rsqrt(jnp.sum(diagonal, axis=0, keepdims=True) + 1e-06)
    similarity = total * inv_col * inv_row
    rank = wide_ref[pl.ds(depth - 2, clusters, stride=depth), :] * RANK_BASE
    rank = rank + wide_ref[pl.ds(depth - 1, clusters, stride=depth), :]
    rank_row = jnp.transpose(rank)[0:1, :]
    allowed = rank[:, 0:1] < rank_row
    best = jnp.max(jnp.where(allowed, similarity, -2.0), axis=0, keepdims=True)
    best = jnp.maximum(best, -1.0)
    lane = iota(out_ref.shape, 1)
    result = jnp.zeros(out_ref.shape, F32)
    for s in range(SLOTS):
        wanted = (iota(size, 0) // SLOTS) * SLOTS + s
        mine = jnp.max(jnp.where(iota(size, 1) == wanted, best, -4.0), axis=1, keepdims=True)
        result = jnp.where(lane == s, mine, result)
    out_ref[...] = result


def owner_best(gain, got, projects, weights, clusters):
    kv_part, width = weights[0].shape
    height = kv_part * SLOTS
    hbm = pl.BlockSpec(memory_space=pl.ANY)
    vmem = pl.BlockSpec(memory_space=pltpu.VMEM)
    return pl.pallas_call(
        owner_kernel,
        in_specs=[vmem] + [hbm] * (1 + len(projects) + len(weights)),
        out_specs=vmem,
        out_shape=jax.ShapeDtypeStruct((clusters, LANES), F32),
        scratch_shapes=[
            pltpu.VMEM(got.shape, BF16),
            pltpu.VMEM(got.shape, F32),
            pltpu.VMEM((clusters, width), BF16),
            pltpu.VMEM((clusters, width), BF16),
            pltpu.VMEM((PROJECT_PARTS, width // PROJECT_PARTS, height), BF16),
            pltpu.VMEM((height, width), BF16),
            pltpu.VMEM((clusters, width), BF16),
            pltpu.VMEM((clusters, width), BF16),
            pltpu.VMEM((clusters, clusters), F32),
            pltpu.VMEM((clusters, clusters), F32),
            pltpu.VMEM((clusters, height), F32),
            pltpu.SemaphoreType.DMA((ROW_PARTS,)),
            pltpu.SemaphoreType.DMA((PROJECT_PARTS, SLOTS)),
            pltpu.SemaphoreType.DMA((OWNER_PARTS, len(weights))),
        ],
        compiler_params=pltpu.CompilerParams(vmem_limit_bytes=58 * MIB),
        cost_estimate=pl.CostEstimate(
            flops=6 * clusters * height * width, bytes_accessed=20 * MIB, transcendentals=0
        ),
        name="owner_best",
    )(gain, got, *projects, *weights)


def pick_kernel(flat_ref, best_ref, out_ref):
    clusters = best_ref.shape[0]
    flat = flat_ref[0:1, :]
    result = jnp.zeros((1, flat.shape[1]), F32)
    for s in range(SLOTS):
        held = jnp.where(chosen(flat, clusters, s), best_ref[:, s : s + 1], 0.0)
        result = result + jnp.sum(held, axis=0, keepdims=True)
    out_ref[...] = result


def pick(flat, best):
    vmem = pl.BlockSpec(memory_space=pltpu.VMEM)
    return pl.pallas_call(
        pick_kernel,
        in_specs=[vmem, vmem],
        out_specs=vmem,
        out_shape=jax.ShapeDtypeStruct((1, flat.shape[1]), F32),
        name="pick",
    )(flat, best)


def ring_pairs(splits, owners):
    cores = 2
    low = splits // cores
    length = 2 * low
    pairs = []
    for d in range(owners):
        for t in range(splits):
            x = (d % 2) * low + t // cores
            to = (x + (1 if t % cores == 0 else -1)) % length
            other = (d // 2 * 2 + to // low) * splits + (to % low) * cores + t % cores
            pairs.append((d * splits + t, other))
    return pairs


def column_pairs(splits, owners):
    pairs = []
    for d in range(owners):
        for t in range(splits):
            y = (d // 2) % 4
            to = (y + (1 if t % 2 == 0 else -1)) % 4
            pairs.append((d * splits + t, (d + (to - y) * 2) * splits + t))
    return pairs


def spread_halves(part, half, splits, owners):
    swap = [(t, t ^ 1) for t in range(splits)]
    near = lax.ppermute(half, AXES, ring_pairs(splits, owners))
    far = lax.ppermute(near, AXES, column_pairs(splits, owners))
    beside = lax.ppermute(part, "tensor", swap)
    return [part, beside, near, far, lax.ppermute(near, "tensor", swap), lax.ppermute(far, "tensor", swap)]


def shards(final_input, norm_gain, value_weight, out_weight, cluster, priority):
    rows, width = final_input.shape
    splits = lax.axis_size("tensor")
    owners = lax.axis_size("dp")
    clusters = splits * owners
    depth = blocks(width) + 2
    flat, message, half = pack(
        cluster.reshape(1, rows),
        priority.reshape(1, rows),
        final_input,
        value_weight,
        clusters,
        depth,
        owners * rows,
    )
    projects = spread_halves(value_weight, half, splits, owners)
    got = lax.all_to_all(message.reshape(clusters, depth // 2, 2, LANES), AXES, 0, 0, tiled=True)
    got = got.reshape(clusters * depth, LANES)
    out_weight, _, _ = lax.optimization_barrier((out_weight, flat, projects[2]))
    folded, folded_half = fold(out_weight)
    weights = spread_halves(folded, folded_half, splits, owners)
    best = owner_best(norm_gain.reshape(blocks(width), LANES), got, projects, weights, clusters)
    returned = lax.all_to_all(best, AXES, 0, 0, tiled=True)
    return pick(flat, returned).reshape(rows)


def solution(mesh):
    in_specs = (P("dp", None), P(), P(None, "tensor"), P("tensor", None), P("dp", None), P("dp"))
    return jax.shard_map(shards, mesh=mesh, in_specs=in_specs, out_specs=P("dp"), check_vma=False)
```

```python
import functools

import jax
import jax.numpy as jnp
from jax import lax
from jax.experimental import pallas as pl
from jax.experimental.pallas import tpu as pltpu
from jax.sharding import PartitionSpec as P

HEADS = 32
KV_HEADS = 8
HEAD_DIM = 128
SLOTS = 4
LANES = 128
AXES = ("dp", "tensor")
F32 = jnp.float32
BF16 = jnp.bfloat16
MIB = 2**20
COLUMN_PARTS = 2
ROW_PARTS = 4
OWNER_PARTS = 4
PROJECT_PARTS = 4
AHEAD = 3
FOLD_PARTS = 4
FOLD_LIMIT = 12
RANK_BASE = 128


def iota(shape, dim):
    return lax.broadcasted_iota(jnp.int32, shape, dim)


def chosen(flat_row, clusters, slot):
    rows = flat_row.shape[1]
    wanted = iota((clusters, rows), 0) * SLOTS + slot
    return flat_row == wanted


def blocks(width):
    return width // LANES


def row_parity():
    return (lax.axis_index("dp").astype(jnp.int32) // 2) % 2


def pack_kernel(
    sentinel, cluster_ref, priority_ref, x_hbm, project_hbm, flat_ref, message_ref, half_hbm, x_ref, wide_ref, half_ref, sems,
):
    rows, width = x_ref.shape
    part = width // COLUMN_PARTS
    x_copies = []
    for j in range(COLUMN_PARTS):
        cols = pl.ds(j * part, part)
        copy = pltpu.make_async_copy(x_hbm.at[:, cols], x_ref.at[:, cols], sems.at[j])
        copy.start()
        x_copies.append(copy)
    half = half_hbm.shape[0]
    start = pl.multiple_of(row_parity() * half, half)
    half_in = pltpu.make_async_copy(project_hbm.at[pl.ds(start, half), :], half_ref, sems.at[COLUMN_PARTS])
    half_in.start()

    me = lax.axis_index("tensor").astype(jnp.int32)
    ids_row = cluster_ref[...]
    ids = jnp.transpose(jnp.broadcast_to(ids_row, (LANES, rows)))[:, 0:1]
    earlier = (ids == ids_row) & (iota((rows, rows), 0) < iota((rows, rows), 1))
    slot = jnp.sum(jnp.where(earlier, 1, 0), axis=0, keepdims=True)
    flat = ids_row * SLOTS + slot
    flat_ref[...] = jnp.broadcast_to(flat, flat_ref.shape)
    depth = blocks(width) + 2
    clusters = wide_ref.shape[0] // depth

    def put(k, block):
        wide_ref[pl.ds(k, clusters, stride=depth), :] = block

    mine = chosen(flat, clusters, me)
    held = jnp.where(mine, priority_ref[...] - sentinel, 0)
    rank = jnp.sum(held, axis=1, keepdims=True) + sentinel
    rank = jnp.broadcast_to(rank, (clusters, LANES))
    put(depth - 2, (rank // RANK_BASE).astype(F32))
    put(depth - 1, (rank % RANK_BASE).astype(F32))

    select = jnp.where(mine, 1.0, 0.0).astype(BF16)
    half_out = pltpu.make_async_copy(half_ref, half_hbm, sems.at[COLUMN_PARTS + 1])
    for j in range(COLUMN_PARTS):
        x_copies[j].wait()
        if j == COLUMN_PARTS - 1:
            half_in.wait()
            half_out.start()
        for k in range(j * part // LANES, (j + 1) * part // LANES, 2):
            picked = jnp.dot(select, x_ref[:, k * LANES : (k + 2) * LANES], preferred_element_type=F32)
            put(k, picked[:, :LANES])
            put(k + 1, picked[:, LANES:])

    share = wide_ref.shape[0] // ROW_PARTS
    for q in range(ROW_PARTS):
        span = pl.ds(q * share, share)
        message_ref[span, :] = wide_ref[span, :].astype(BF16)
    half_out.wait()


def pack(cluster, priority, x, project, clusters, depth, sentinel):
    rows, width = x.shape
    hbm = pl.BlockSpec(memory_space=pl.ANY)
    vmem = pl.BlockSpec(memory_space=pltpu.VMEM)
    return pl.pallas_call(
        functools.partial(pack_kernel, sentinel),
        in_specs=[vmem, vmem, hbm, hbm],
        out_specs=[vmem, vmem, hbm],
        out_shape=[
            jax.ShapeDtypeStruct((8, rows), jnp.int32),
            pltpu.VMEM((clusters * depth, LANES), BF16),
            jax.ShapeDtypeStruct((project.shape[0] // 2, project.shape[1]), BF16),
        ],
        scratch_shapes=[
            pltpu.VMEM((rows, width), BF16),
            pltpu.VMEM((clusters * depth, LANES), F32),
            pltpu.VMEM((project.shape[0] // 2, project.shape[1]), BF16),
            pltpu.SemaphoreType.DMA((COLUMN_PARTS + 2,)),
        ],
        compiler_params=pltpu.CompilerParams(vmem_limit_bytes=58 * MIB),
        cost_estimate=pl.CostEstimate(
            flops=2 * clusters * rows * width, bytes_accessed=3 * rows * width, transcendentals=0
        ),
        name="pack",
    )(cluster, priority, x, project)


def fold_kernel(near, weight_hbm, out_hbm, weight_ref, out_ref, in_sems, out_sems):
    group, width = HEADS // KV_HEADS, out_ref.shape[1]
    height = weight_ref.shape[0]
    chosen_half = row_parity() if near else 1 - row_parity()
    begin = pl.multiple_of(chosen_half * height, height)
    part = width // FOLD_PARTS
    in_copies = []
    for j in range(FOLD_PARTS):
        cols = pl.ds(j * part, part)
        copy = pltpu.make_async_copy(
            weight_hbm.at[pl.ds(begin, height), cols], weight_ref.at[:, cols], in_sems.at[j]
        )
        copy.start()
        in_copies.append(copy)
    out_copies = []
    for j in range(FOLD_PARTS):
        in_copies[j].wait()
        cols = slice(j * part, (j + 1) * part)
        total = 0.0
        for g in range(group):
            total = total + weight_ref[g * HEAD_DIM : (g + 1) * HEAD_DIM, cols].astype(F32)
        out_ref[:, cols] = total.astype(BF16)
        span = pl.ds(j * part, part)
        copy = pltpu.make_async_copy(out_ref.at[:, span], out_hbm.at[:, span], out_sems.at[j])
        copy.start()
        out_copies.append(copy)
    for copy in out_copies:
        copy.wait()


def fold(out_weight, near):
    height, width = out_weight.shape
    hbm = pl.BlockSpec(memory_space=pl.ANY)
    return pl.pallas_call(
        functools.partial(fold_kernel, near),
        in_specs=[hbm],
        out_specs=hbm,
        out_shape=jax.ShapeDtypeStruct((HEAD_DIM, width), BF16),
        scratch_shapes=[
            pltpu.VMEM((height // 2, width), BF16),
            pltpu.VMEM((HEAD_DIM, width), BF16),
            pltpu.SemaphoreType.DMA((FOLD_PARTS,)),
            pltpu.SemaphoreType.DMA((FOLD_PARTS,)),
        ],
        compiler_params=pltpu.CompilerParams(vmem_limit_bytes=FOLD_LIMIT * MIB),
        cost_estimate=pl.CostEstimate(
            flops=4 * 10**11 if near else 4 * MIB, bytes_accessed=5 * MIB, transcendentals=0
        ),
        name="fold_near" if near else "fold_far",
    )(pltpu.with_memory_space_constraint(out_weight, pltpu.MemorySpace.HBM))


def owner_kernel(
    gain_ref, got_hbm, v0, v1, v2, v2y, v3, v3y, w0, w0y, w1, w1y, w2, w2y, w3, w3y, out_ref,
    got_ref, wide_ref, x_ref, gained_ref, project_ref, weight_ref, high, low, gram_ref, cross_ref, product_ref,
    got_sems, project_sems, weight_sems,
):
    clusters, width = high.shape
    depth = got_ref.shape[0] // clusters
    kv_part = v0.shape[1]
    share = got_ref.shape[0] // ROW_PARTS
    got_copies = []
    for q in range(ROW_PARTS):
        span = pl.ds(q * share, share)
        got_copies.append(pltpu.make_async_copy(got_hbm.at[span, :], got_ref.at[span, :], got_sems.at[q]))
    half = v2.shape[0]
    near = row_parity() * half
    far = half - near
    step = 2 * half // PROJECT_PARTS
    starts = []
    project_groups = []
    for p in range(PROJECT_PARTS):
        inner = p * step % half
        begin = pl.multiple_of((near if p * step < half else far) + inner, step)
        starts.append(begin)
        third, fourth = (v2, v3) if p * step < half else (v2y, v3y)
        project_groups.append(
            [
                pltpu.make_async_copy(
                    source.at[pl.ds(first, step), :],
                    project_ref.at[p, :, pl.ds(n * kv_part, kv_part)],
                    project_sems.at[p, n],
                )
                for n, (source, first) in enumerate(((v0, begin), (v1, begin), (third, inner), (fourth, inner)))
            ]
        )
    part = width // OWNER_PARTS
    rows = w2.shape[0]
    near = row_parity() * rows
    far = rows - near
    weight_groups = []
    for j in range(OWNER_PARTS):
        cols = pl.ds(j * part, part)
        group = []
        for i, source in enumerate((w0, w0y, w1, w1y, w2, w2y, w3, w3y)):
            shift = near if i % 2 == 0 else far
            span = pl.ds(pl.multiple_of(i // 2 * kv_part + shift, rows), rows)
            group.append(
                pltpu.make_async_copy(source.at[:, cols], weight_ref.at[span, cols], weight_sems.at[j, i])
            )
        weight_groups.append(group)
    groups = project_groups + weight_groups

    def start(n):
        if n < len(groups):
            for copy in groups[n]:
                copy.start()

    for copy in got_copies:
        copy.start()
    for q in range(ROW_PARTS):
        span = pl.ds(q * share, share)
        got_copies[q].wait()
        if q >= ROW_PARTS - AHEAD:
            start(q - ROW_PARTS + AHEAD)
        wide_ref[span, :] = got_ref[span, :].astype(F32)
    gain = gain_ref[...].astype(F32)
    squares = jnp.zeros((clusters, LANES), F32)
    for k in range(blocks(width)):
        cols = slice(k * LANES, (k + 1) * LANES)
        block = wide_ref[pl.ds(k, clusters, stride=depth), :]
        squares = squares + block * block
        x_ref[:, cols] = block.astype(BF16)
        gained_ref[:, cols] = (block * gain[k : k + 1, :]).astype(BF16)
    for p in range(PROJECT_PARTS):
        for copy in project_groups[p]:
            copy.wait()
        start(p + AHEAD)
        product = jnp.dot(
            gained_ref[:, pl.ds(starts[p], step)], project_ref[p], preferred_element_type=F32
        )
        product_ref[...] = product if p == 0 else product_ref[...] + product
    scale = lax.rsqrt(jnp.sum(squares, axis=1, keepdims=True) / width + 1e-05)
    values = (product_ref[...] * scale).astype(BF16)
    contract = (((1,), (1,)), ((), ()))
    for j in range(OWNER_PARTS):
        for copy in weight_groups[j]:
            copy.wait()
        start(PROJECT_PARTS + j + AHEAD)
        for k in range(j * part // LANES, (j + 1) * part // LANES, 2):
            cols = slice(k * LANES, (k + 2) * LANES)
            hidden = x_ref[:, cols].astype(F32) + jnp.dot(
                values, weight_ref[:, cols], preferred_element_type=F32
            )
            upper = hidden.astype(BF16)
            high[:, cols] = upper
            low[:, cols] = (hidden - upper.astype(F32)).astype(BF16)
        cols = slice(j * part, (j + 1) * part)
        gram = lax.dot_general(high[:, cols], high[:, cols], contract, preferred_element_type=F32)
        cross = lax.dot_general(high[:, cols], low[:, cols], contract, preferred_element_type=F32)
        gram_ref[...] = gram if j == 0 else gram_ref[...] + gram
        cross_ref[...] = cross if j == 0 else cross_ref[...] + cross

    gram = gram_ref[...]
    cross = cross_ref[...]
    total = gram + (cross + jnp.transpose(cross))
    size = (clusters, clusters)
    diagonal = jnp.where(iota(size, 0) == iota(size, 1), total, 0.0)
    inv_col = lax.rsqrt(jnp.sum(diagonal, axis=1, keepdims=True) + 1e-06)
    inv_row = lax.rsqrt(jnp.sum(diagonal, axis=0, keepdims=True) + 1e-06)
    similarity = total * inv_col * inv_row
    rank = wide_ref[pl.ds(depth - 2, clusters, stride=depth), :] * RANK_BASE
    rank = rank + wide_ref[pl.ds(depth - 1, clusters, stride=depth), :]
    rank_row = jnp.transpose(rank)[0:1, :]
    allowed = rank[:, 0:1] < rank_row
    best = jnp.max(jnp.where(allowed, similarity, -2.0), axis=0, keepdims=True)
    best = jnp.maximum(best, -1.0)
    lane = iota(out_ref.shape, 1)
    result = jnp.zeros(out_ref.shape, F32)
    for s in range(SLOTS):
        wanted = (iota(size, 0) // SLOTS) * SLOTS + s
        mine = jnp.max(jnp.where(iota(size, 1) == wanted, best, -4.0), axis=1, keepdims=True)
        result = jnp.where(lane == s, mine, result)
    out_ref[...] = result


def owner_best(gain, got, projects, weights, clusters):
    width, kv_part = projects[0].shape
    height = kv_part * SLOTS
    hbm = pl.BlockSpec(memory_space=pl.ANY)
    vmem = pl.BlockSpec(memory_space=pltpu.VMEM)
    return pl.pallas_call(
        owner_kernel,
        in_specs=[vmem] + [hbm] * (1 + len(projects) + len(weights)),
        out_specs=vmem,
        out_shape=jax.ShapeDtypeStruct((clusters, LANES), F32),
        scratch_shapes=[
            pltpu.VMEM(got.shape, BF16),
            pltpu.VMEM(got.shape, F32),
            pltpu.VMEM((clusters, width), BF16),
            pltpu.VMEM((clusters, width), BF16),
            pltpu.VMEM((PROJECT_PARTS, width // PROJECT_PARTS, height), BF16),
            pltpu.VMEM((height, width), BF16),
            pltpu.VMEM((clusters, width), BF16),
            pltpu.VMEM((clusters, width), BF16),
            pltpu.VMEM((clusters, clusters), F32),
            pltpu.VMEM((clusters, clusters), F32),
            pltpu.VMEM((clusters, height), F32),
            pltpu.SemaphoreType.DMA((ROW_PARTS,)),
            pltpu.SemaphoreType.DMA((PROJECT_PARTS, SLOTS)),
            pltpu.SemaphoreType.DMA((OWNER_PARTS, len(weights))),
        ],
        compiler_params=pltpu.CompilerParams(vmem_limit_bytes=58 * MIB),
        cost_estimate=pl.CostEstimate(
            flops=6 * clusters * height * width, bytes_accessed=20 * MIB, transcendentals=0
        ),
        name="owner_best",
    )(gain, got, *projects, *weights)


def pick_kernel(flat_ref, best_ref, out_ref):
    clusters = best_ref.shape[0]
    flat = flat_ref[0:1, :]
    result = jnp.zeros((1, flat.shape[1]), F32)
    for s in range(SLOTS):
        held = jnp.where(chosen(flat, clusters, s), best_ref[:, s : s + 1], 0.0)
        result = result + jnp.sum(held, axis=0, keepdims=True)
    out_ref[...] = result


def pick(flat, best):
    vmem = pl.BlockSpec(memory_space=pltpu.VMEM)
    return pl.pallas_call(
        pick_kernel,
        in_specs=[vmem, vmem],
        out_specs=vmem,
        out_shape=jax.ShapeDtypeStruct((1, flat.shape[1]), F32),
        name="pick",
    )(flat, best)


def ring_pairs(splits, owners):
    cores = 2
    low = splits // cores
    length = 2 * low
    pairs = []
    for d in range(owners):
        for t in range(splits):
            x = (d % 2) * low + t // cores
            to = (x + (1 if t % cores == 0 else -1)) % length
            other = (d // 2 * 2 + to // low) * splits + (to % low) * cores + t % cores
            pairs.append((d * splits + t, other))
    return pairs


def column_pairs(splits, owners):
    pairs = []
    for d in range(owners):
        for t in range(splits):
            y = (d // 2) % 4
            to = (y + (1 if t % 2 == 0 else -1)) % 4
            pairs.append((d * splits + t, (d + (to - y) * 2) * splits + t))
    return pairs


def cross(near, splits, owners):
    swap = [(t, t ^ 1) for t in range(splits)]
    across = lax.ppermute(near, AXES, ring_pairs(splits, owners))
    along = lax.ppermute(across, AXES, column_pairs(splits, owners))
    return [across, along, lax.ppermute(across, "tensor", swap), lax.ppermute(along, "tensor", swap)]


def shards(final_input, norm_gain, value_weight, out_weight, cluster, priority):
    rows, width = final_input.shape
    splits = lax.axis_size("tensor")
    owners = lax.axis_size("dp")
    clusters = splits * owners
    depth = blocks(width) + 2
    flat, message, half = pack(
        cluster.reshape(1, rows),
        priority.reshape(1, rows),
        final_input,
        value_weight,
        clusters,
        depth,
        owners * rows,
    )
    swap = [(t, t ^ 1) for t in range(splits)]
    projects = [value_weight, lax.ppermute(value_weight, "tensor", swap), *cross(half, splits, owners)]
    got = lax.all_to_all(message.reshape(clusters, depth // 2, 2, LANES), AXES, 0, 0, tiled=True)
    got = got.reshape(clusters * depth, LANES)
    out_weight, _, _ = lax.optimization_barrier((out_weight, flat, projects[2]))
    near = fold(out_weight, True)
    out_weight, near = lax.optimization_barrier((out_weight, near))
    far = fold(out_weight, False)
    beside = [lax.ppermute(w, "tensor", swap) for w in (near, far)]
    weights = [near, far, *beside, *cross(near, splits, owners)]
    best = owner_best(norm_gain.reshape(blocks(width), LANES), got, projects, weights, clusters)
    returned = lax.all_to_all(best, AXES, 0, 0, tiled=True)
    return pick(flat, returned).reshape(rows)


def solution(mesh):
    in_specs = (P("dp", None), P(), P(None, "tensor"), P("tensor", None), P("dp", None), P("dp"))
    return jax.shard_map(shards, mesh=mesh, in_specs=in_specs, out_specs=P("dp"), check_vma=False)
```

```python
import functools

import jax
import jax.numpy as jnp
from jax import lax
from jax.experimental import pallas as pl
from jax.experimental.pallas import tpu as pltpu
from jax.sharding import PartitionSpec as P

HEADS = 32
KV_HEADS = 8
HEAD_DIM = 128
SLOTS = 4
LANES = 128
AXES = ("dp", "tensor")
F32 = jnp.float32
BF16 = jnp.bfloat16
MIB = 2**20
COLUMN_PARTS = 2
ROW_PARTS = 4
OWNER_PARTS = 4
PROJECT_PARTS = 4
AHEAD = 3
FOLD_PARTS = 4
FOLD_LIMIT = 12
RANK_BASE = 128


def iota(shape, dim):
    return lax.broadcasted_iota(jnp.int32, shape, dim)


def chosen(flat_row, clusters, slot):
    rows = flat_row.shape[1]
    wanted = iota((clusters, rows), 0) * SLOTS + slot
    return flat_row == wanted


def blocks(width):
    return width // LANES


def row_parity():
    return (lax.axis_index("dp").astype(jnp.int32) // 2) % 2


def pack_kernel(
    sentinel, cluster_ref, priority_ref, x_hbm, project_hbm, flat_ref, message_ref, half_hbm, x_ref, wide_ref, half_ref, sems,
):
    rows, width = x_ref.shape
    part = width // COLUMN_PARTS
    x_copies = []
    for j in range(COLUMN_PARTS):
        cols = pl.ds(j * part, part)
        copy = pltpu.make_async_copy(x_hbm.at[:, cols], x_ref.at[:, cols], sems.at[j])
        copy.start()
        x_copies.append(copy)
    half = half_hbm.shape[0]
    start = pl.multiple_of(row_parity() * half, half)
    half_in = pltpu.make_async_copy(project_hbm.at[pl.ds(start, half), :], half_ref, sems.at[COLUMN_PARTS])
    half_in.start()

    me = lax.axis_index("tensor").astype(jnp.int32)
    ids_row = cluster_ref[...]
    ids = jnp.transpose(jnp.broadcast_to(ids_row, (LANES, rows)))[:, 0:1]
    earlier = (ids == ids_row) & (iota((rows, rows), 0) < iota((rows, rows), 1))
    slot = jnp.sum(jnp.where(earlier, 1, 0), axis=0, keepdims=True)
    flat = ids_row * SLOTS + slot
    flat_ref[...] = jnp.broadcast_to(flat, flat_ref.shape)
    depth = blocks(width) + 2
    clusters = wide_ref.shape[0] // depth

    def put(k, block):
        wide_ref[pl.ds(k, clusters, stride=depth), :] = block

    mine = chosen(flat, clusters, me)
    held = jnp.where(mine, priority_ref[...] - sentinel, 0)
    rank = jnp.sum(held, axis=1, keepdims=True) + sentinel
    rank = jnp.broadcast_to(rank, (clusters, LANES))
    put(depth - 2, (rank // RANK_BASE).astype(F32))
    put(depth - 1, (rank % RANK_BASE).astype(F32))

    select = jnp.where(mine, 1.0, 0.0).astype(BF16)
    half_out = pltpu.make_async_copy(half_ref, half_hbm, sems.at[COLUMN_PARTS + 1])
    for j in range(COLUMN_PARTS):
        x_copies[j].wait()
        if j == COLUMN_PARTS - 1:
            half_in.wait()
            half_out.start()
        for k in range(j * part // LANES, (j + 1) * part // LANES, 2):
            picked = jnp.dot(select, x_ref[:, k * LANES : (k + 2) * LANES], preferred_element_type=F32)
            put(k, picked[:, :LANES])
            put(k + 1, picked[:, LANES:])

    share = wide_ref.shape[0] // ROW_PARTS
    for q in range(ROW_PARTS):
        span = pl.ds(q * share, share)
        message_ref[span, :] = wide_ref[span, :].astype(BF16)
    half_out.wait()


def pack(cluster, priority, x, project, clusters, depth, sentinel):
    rows, width = x.shape
    hbm = pl.BlockSpec(memory_space=pl.ANY)
    vmem = pl.BlockSpec(memory_space=pltpu.VMEM)
    return pl.pallas_call(
        functools.partial(pack_kernel, sentinel),
        in_specs=[vmem, vmem, hbm, hbm],
        out_specs=[vmem, vmem, hbm],
        out_shape=[
            jax.ShapeDtypeStruct((8, rows), jnp.int32),
            pltpu.VMEM((clusters * depth, LANES), BF16),
            jax.ShapeDtypeStruct((project.shape[0] // 2, project.shape[1]), BF16),
        ],
        scratch_shapes=[
            pltpu.VMEM((rows, width), BF16),
            pltpu.VMEM((clusters * depth, LANES), F32),
            pltpu.VMEM((project.shape[0] // 2, project.shape[1]), BF16),
            pltpu.SemaphoreType.DMA((COLUMN_PARTS + 2,)),
        ],
        compiler_params=pltpu.CompilerParams(vmem_limit_bytes=58 * MIB),
        cost_estimate=pl.CostEstimate(
            flops=2 * clusters * rows * width, bytes_accessed=3 * rows * width, transcendentals=0
        ),
        name="pack",
    )(cluster, priority, x, project)


def fold_kernel(near, weight_hbm, out_hbm, weight_ref, out_ref, in_sems, out_sems):
    group, width = HEADS // KV_HEADS, out_ref.shape[1]
    height = weight_ref.shape[0]
    chosen_half = row_parity() if near else 1 - row_parity()
    begin = pl.multiple_of(chosen_half * height, height)
    part = width // FOLD_PARTS
    in_copies = []
    for j in range(FOLD_PARTS):
        cols = pl.ds(j * part, part)
        copy = pltpu.make_async_copy(
            weight_hbm.at[pl.ds(begin, height), cols], weight_ref.at[:, cols], in_sems.at[j]
        )
        copy.start()
        in_copies.append(copy)
    out_copies = []
    for j in range(FOLD_PARTS):
        in_copies[j].wait()
        cols = slice(j * part, (j + 1) * part)
        total = 0.0
        for g in range(group):
            total = total + weight_ref[g * HEAD_DIM : (g + 1) * HEAD_DIM, cols].astype(F32)
        out_ref[:, cols] = total.astype(BF16)
        span = pl.ds(j * part, part)
        copy = pltpu.make_async_copy(out_ref.at[:, span], out_hbm.at[:, span], out_sems.at[j])
        copy.start()
        out_copies.append(copy)
    for copy in out_copies:
        copy.wait()


def fold(out_weight, near):
    height, width = out_weight.shape
    hbm = pl.BlockSpec(memory_space=pl.ANY)
    return pl.pallas_call(
        functools.partial(fold_kernel, near),
        in_specs=[hbm],
        out_specs=hbm,
        out_shape=jax.ShapeDtypeStruct((HEAD_DIM, width), BF16),
        scratch_shapes=[
            pltpu.VMEM((height // 2, width), BF16),
            pltpu.VMEM((HEAD_DIM, width), BF16),
            pltpu.SemaphoreType.DMA((FOLD_PARTS,)),
            pltpu.SemaphoreType.DMA((FOLD_PARTS,)),
        ],
        compiler_params=pltpu.CompilerParams(vmem_limit_bytes=FOLD_LIMIT * MIB),
        cost_estimate=pl.CostEstimate(
            flops=4 * 10**11 if near else 4 * MIB, bytes_accessed=5 * MIB, transcendentals=0
        ),
        name="fold_near" if near else "fold_far",
    )(pltpu.with_memory_space_constraint(out_weight, pltpu.MemorySpace.HBM))


def owner_kernel(
    gain_ref, got_hbm, v0, v1, v2, v2y, v3, v3y, w0, w0y, w1, w1y, w2, w2y, w3, w3y, out_ref,
    got_ref, wide_ref, x_ref, gained_ref, project_ref, weight_ref, high, low, gram_ref, cross_ref, product_ref,
    got_sems, project_sems, weight_sems,
):
    clusters, width = high.shape
    depth = got_ref.shape[0] // clusters
    kv_part = v0.shape[1]
    share = got_ref.shape[0] // ROW_PARTS
    got_copies = []
    for q in range(ROW_PARTS):
        span = pl.ds(q * share, share)
        got_copies.append(pltpu.make_async_copy(got_hbm.at[span, :], got_ref.at[span, :], got_sems.at[q]))
    half = v2.shape[0]
    near = row_parity() * half
    far = half - near
    step = 2 * half // PROJECT_PARTS
    starts = []
    project_groups = []
    for p in range(PROJECT_PARTS):
        inner = p * step % half
        begin = pl.multiple_of((near if p * step < half else far) + inner, step)
        starts.append(begin)
        third, fourth = (v2, v3) if p * step < half else (v2y, v3y)
        project_groups.append(
            [
                pltpu.make_async_copy(
                    source.at[pl.ds(first, step), :],
                    project_ref.at[p, :, pl.ds(n * kv_part, kv_part)],
                    project_sems.at[p, n],
                )
                for n, (source, first) in enumerate(((v0, begin), (v1, begin), (third, inner), (fourth, inner)))
            ]
        )
    part = width // OWNER_PARTS
    rows = w2.shape[0]
    near = row_parity() * rows
    far = rows - near
    weight_groups = []
    for j in range(OWNER_PARTS):
        cols = pl.ds(j * part, part)
        group = []
        for i, source in enumerate((w0, w0y, w1, w1y, w2, w2y, w3, w3y)):
            shift = near if i % 2 == 0 else far
            span = pl.ds(pl.multiple_of(i // 2 * kv_part + shift, rows), rows)
            group.append(
                pltpu.make_async_copy(source.at[:, cols], weight_ref.at[span, cols], weight_sems.at[j, i])
            )
        weight_groups.append(group)
    groups = project_groups + weight_groups

    def start(n):
        if n < len(groups):
            for copy in groups[n]:
                copy.start()

    for copy in got_copies:
        copy.start()
    for q in range(ROW_PARTS):
        span = pl.ds(q * share, share)
        got_copies[q].wait()
        if q >= ROW_PARTS - AHEAD:
            start(q - ROW_PARTS + AHEAD)
        wide_ref[span, :] = got_ref[span, :].astype(F32)
    gain = gain_ref[...].astype(F32)
    squares = jnp.zeros((clusters, LANES), F32)
    for k in range(blocks(width)):
        cols = slice(k * LANES, (k + 1) * LANES)
        block = wide_ref[pl.ds(k, clusters, stride=depth), :]
        squares = squares + block * block
        x_ref[:, cols] = block.astype(BF16)
        gained_ref[:, cols] = (block * gain[k : k + 1, :]).astype(BF16)
    for p in range(PROJECT_PARTS):
        for copy in project_groups[p]:
            copy.wait()
        start(p + AHEAD)
        product = jnp.dot(
            gained_ref[:, pl.ds(starts[p], step)], project_ref[p], preferred_element_type=F32
        )
        product_ref[...] = product if p == 0 else product_ref[...] + product
    scale = lax.rsqrt(jnp.sum(squares, axis=1, keepdims=True) / width + 1e-05)
    values = (product_ref[...] * scale).astype(BF16)
    contract = (((1,), (1,)), ((), ()))
    for j in range(OWNER_PARTS):
        for copy in weight_groups[j]:
            copy.wait()
        start(PROJECT_PARTS + j + AHEAD)
        for k in range(j * part // LANES, (j + 1) * part // LANES, 2):
            cols = slice(k * LANES, (k + 2) * LANES)
            hidden = x_ref[:, cols].astype(F32) + jnp.dot(
                values, weight_ref[:, cols], preferred_element_type=F32
            )
            upper = hidden.astype(BF16)
            high[:, cols] = upper
            low[:, cols] = (hidden - upper.astype(F32)).astype(BF16)
        cols = slice(j * part, (j + 1) * part)
        gram = lax.dot_general(high[:, cols], high[:, cols], contract, preferred_element_type=F32)
        cross = lax.dot_general(high[:, cols], low[:, cols], contract, preferred_element_type=F32)
        gram_ref[...] = gram if j == 0 else gram_ref[...] + gram
        cross_ref[...] = cross if j == 0 else cross_ref[...] + cross

    gram = gram_ref[...]
    cross = cross_ref[...]
    total = gram + (cross + jnp.transpose(cross))
    size = (clusters, clusters)
    diagonal = jnp.where(iota(size, 0) == iota(size, 1), total, 0.0)
    inv_col = lax.rsqrt(jnp.sum(diagonal, axis=1, keepdims=True) + 1e-06)
    inv_row = lax.rsqrt(jnp.sum(diagonal, axis=0, keepdims=True) + 1e-06)
    similarity = total * inv_col * inv_row
    rank = wide_ref[pl.ds(depth - 2, clusters, stride=depth), :] * RANK_BASE
    rank = rank + wide_ref[pl.ds(depth - 1, clusters, stride=depth), :]
    rank_row = jnp.transpose(rank)[0:1, :]
    allowed = rank[:, 0:1] < rank_row
    best = jnp.max(jnp.where(allowed, similarity, -2.0), axis=0, keepdims=True)
    best = jnp.maximum(best, -1.0)
    lane = iota(out_ref.shape, 1)
    result = jnp.zeros(out_ref.shape, F32)
    for s in range(SLOTS):
        wanted = (iota(size, 0) // SLOTS) * SLOTS + s
        mine = jnp.max(jnp.where(iota(size, 1) == wanted, best, -4.0), axis=1, keepdims=True)
        result = jnp.where(lane == s, mine, result)
    out_ref[...] = result


def owner_best(gain, got, projects, weights, clusters):
    width, kv_part = projects[0].shape
    height = kv_part * SLOTS
    hbm = pl.BlockSpec(memory_space=pl.ANY)
    vmem = pl.BlockSpec(memory_space=pltpu.VMEM)
    return pl.pallas_call(
        owner_kernel,
        in_specs=[vmem] + [hbm] * (1 + len(projects) + len(weights)),
        out_specs=vmem,
        out_shape=jax.ShapeDtypeStruct((clusters, LANES), F32),
        scratch_shapes=[
            pltpu.VMEM(got.shape, BF16),
            pltpu.VMEM(got.shape, F32),
            pltpu.VMEM((clusters, width), BF16),
            pltpu.VMEM((clusters, width), BF16),
            pltpu.VMEM((PROJECT_PARTS, width // PROJECT_PARTS, height), BF16),
            pltpu.VMEM((height, width), BF16),
            pltpu.VMEM((clusters, width), BF16),
            pltpu.VMEM((clusters, width), BF16),
            pltpu.VMEM((clusters, clusters), F32),
            pltpu.VMEM((clusters, clusters), F32),
            pltpu.VMEM((clusters, height), F32),
            pltpu.SemaphoreType.DMA((ROW_PARTS,)),
            pltpu.SemaphoreType.DMA((PROJECT_PARTS, SLOTS)),
            pltpu.SemaphoreType.DMA((OWNER_PARTS, len(weights))),
        ],
        compiler_params=pltpu.CompilerParams(vmem_limit_bytes=58 * MIB),
        cost_estimate=pl.CostEstimate(
            flops=6 * clusters * height * width, bytes_accessed=20 * MIB, transcendentals=0
        ),
        name="owner_best",
    )(gain, got, *projects, *weights)


def pick_kernel(flat_ref, best_ref, out_ref):
    clusters = best_ref.shape[0]
    flat = flat_ref[0:1, :]
    result = jnp.zeros((1, flat.shape[1]), F32)
    for s in range(SLOTS):
        held = jnp.where(chosen(flat, clusters, s), best_ref[:, s : s + 1], 0.0)
        result = result + jnp.sum(held, axis=0, keepdims=True)
    out_ref[...] = result


def pick(flat, best):
    vmem = pl.BlockSpec(memory_space=pltpu.VMEM)
    return pl.pallas_call(
        pick_kernel,
        in_specs=[vmem, vmem],
        out_specs=vmem,
        out_shape=jax.ShapeDtypeStruct((1, flat.shape[1]), F32),
        name="pick",
    )(flat, best)


def ring_pairs(splits, owners):
    cores = 2
    low = splits // cores
    length = 2 * low
    pairs = []
    for d in range(owners):
        for t in range(splits):
            x = (d % 2) * low + t // cores
            to = (x + (1 if t % cores == 0 else -1)) % length
            other = (d // 2 * 2 + to // low) * splits + (to % low) * cores + t % cores
            pairs.append((d * splits + t, other))
    return pairs


def column_pairs(splits, owners):
    pairs = []
    for d in range(owners):
        for t in range(splits):
            y = (d // 2) % 4
            to = (y + (1 if t % 2 == 0 else -1)) % 4
            pairs.append((d * splits + t, (d + (to - y) * 2) * splits + t))
    return pairs


def shards(final_input, norm_gain, value_weight, out_weight, cluster, priority):
    rows, width = final_input.shape
    splits = lax.axis_size("tensor")
    owners = lax.axis_size("dp")
    clusters = splits * owners
    depth = blocks(width) + 2
    flat, message, half = pack(
        cluster.reshape(1, rows),
        priority.reshape(1, rows),
        final_input,
        value_weight,
        clusters,
        depth,
        owners * rows,
    )
    swap = [(t, t ^ 1) for t in range(splits)]
    v_across = lax.ppermute(half, AXES, ring_pairs(splits, owners))
    v_along = lax.ppermute(v_across, AXES, column_pairs(splits, owners))
    got = lax.all_to_all(message.reshape(clusters, depth // 2, 2, LANES), AXES, 0, 0, tiled=True)
    got = got.reshape(clusters * depth, LANES)
    out_weight, _, _ = lax.optimization_barrier((out_weight, flat, v_across))
    near = fold(out_weight, True)
    out_weight, near = lax.optimization_barrier((out_weight, near))
    far = fold(out_weight, False)
    beside = [lax.ppermute(w, "tensor", swap) for w in (near, far)]
    across = [lax.ppermute(w, AXES, ring_pairs(splits, owners)) for w in (near, far)]
    across[1], v_along = lax.optimization_barrier((across[1], v_along))
    weights = [near, far, *beside, *across, *[lax.ppermute(w, "tensor", swap) for w in across]]
    projects = [value_weight, lax.ppermute(value_weight, "tensor", swap), v_across, v_along]
    projects += [lax.ppermute(w, "tensor", swap) for w in (v_across, v_along)]
    best = owner_best(norm_gain.reshape(blocks(width), LANES), got, projects, weights, clusters)
    returned = lax.all_to_all(best, AXES, 0, 0, tiled=True)
    return pick(flat, returned).reshape(rows)


def solution(mesh):
    in_specs = (P("dp", None), P(), P(None, "tensor"), P("tensor", None), P("dp", None), P("dp"))
    return jax.shard_map(shards, mesh=mesh, in_specs=in_specs, out_specs=P("dp"), check_vma=False)
```
